256 devices in a mesh: row: 16 (over x_hi, z), col: 16 (over x_lo, y, core).
Axes of the slice: x: 4 (x_hi: 2, x_lo: 2; x = x_hi * 2 + x_lo), y: 4, z: 8, core: 2. Of those that a mesh axis runs over, the one named last changes fastest.
Arguments:
- inputs: bfloat16 [1536, 12288], P('col', 'row'), may hold values from -6 to 6
- grad_out: bfloat16 [1536, 49152], P('row', 'col'), may hold values from -6 to 6
- weight: bfloat16 [12288, 49152], P('row', 'col'), may hold values from -0.02734375 to 0.02734375
Outputs:
- weight_grad: bfloat16 [12288, 49152], P('row', 'col')
- input_grad: bfloat16 [1536, 12288], P('col', 'row')
The draws below stay inside these ranges and needn't reach their ends.
All inputs are finite; a program needn't handle non-finite values.
Results may differ from the reference program's by a relative error of at most 0.001.
Values may be sent and summed in bfloat16 or wider, within the bound.
No kernel may reach another device: no remote copies, remote signals or barrier semaphores. Data moves between devices by JAX's collectives and lax.ppermute only.
A program may use at most 64 MiB of HBM per device.

```python
import jax
import jax.numpy as jnp
from jax import lax

D = 12288
FF = 49152
TOKENS = 1536


def strengthened(result, rng, source, target, shards_of, factor):
    def block_of(axis_at):
        return (jnp.arange(result.shape[axis_at]) // (result.shape[axis_at] // shards_of)).reshape((-1,) + (1,) * (result.ndim - 1 - axis_at))

    near = jax.random.permutation(rng, shards_of)[block_of(target)]
    far = (block_of(target) + shards_of // 2) % shards_of
    return jnp.where((block_of(source) == near) | (block_of(source) == far), factor * result, result)


def block_levels(stream_key, dims, pieces, low, high):
    level, own = 1.0, jax.random.fold_in(stream_key, 6)
    for position, parts in pieces:
        steps = jnp.exp(jax.random.uniform(jax.random.fold_in(own, position), (parts,), jnp.float32, low / len(pieces), high / len(pieces)))
        level = level * jnp.repeat(steps, dims[position] // parts).reshape([-1 if axis == position else 1 for axis in range(len(dims))])
    return level


def gaussian(stream_key, extent, spread, reach, cuts=(), held_as=jnp.bfloat16):
    values = jax.random.normal(stream_key, extent, jnp.float32) * spread
    if len(cuts) > 0:
        values = block_levels(stream_key, extent, cuts, -0.22, 0.18) * values
    return jnp.clip(values, min=-reach, max=reach).astype(held_as)


def noise_with(key, shape, spread, most, pieces, heavy, kind=jnp.bfloat16):
    array = spread * jax.random.normal(key, shape, jnp.float32)
    if pieces:
        array = array * block_levels(key, shape, pieces, -0.22, 0.18)
    return jnp.clip(strengthened(array, jax.random.fold_in(key, 3), *heavy), -most, most).astype(kind)


def setup_inputs(seed: int = 0) -> dict:
    key_of = jax.random.split(jax.random.key(seed), 4)
    return {
        "inputs": gaussian(key_of[0], (TOKENS, D), 1.0, 6.0, ((0, 16), (1, 16))),
        "grad_out": noise_with(key_of[1], (TOKENS, FF), 1.0, 6.0, ((0, 16), (1, 16)), (1, 0, 16, 2.0)),
        "weight": gaussian(key_of[2], (D, FF), FF ** -0.5, 0.02734375, ((0, 16), (1, 16))),
    }


def reference(inputs, grad_out, weight):
    weight_grad = lax.dot_general(inputs, grad_out, (((0,), (0,)), ((), ())), preferred_element_type=jnp.float32)
    input_grad = lax.dot_general(grad_out, weight, (((1,), (1,)), ((), ())), preferred_element_type=jnp.float32)
    return weight_grad.astype(jnp.bfloat16), input_grad.astype(jnp.bfloat16)
```

```python
import jax
import jax.numpy as jnp
from jax import lax
from jax.experimental import pallas as pl
from jax.experimental.pallas import tpu as pltpu
from jax.sharding import PartitionSpec as P

BF16, F32 = jnp.bfloat16, jnp.float32
ARRIVAL = (0, 1, -1, -2, 2, 3, -3, -4)
GROUPS = {"late": (0, 48), "first": (48, 96)}
ORDER = "AbBabBfabBfabBfafB"
IN_FLIGHT = 4
INPUT_TILE, WEIGHT_TILE, VMEM_LIMIT = 768, 512, 40 << 20


def by_row(move):
    return [(r, move(r // 8, r % 8)) for r in range(16)]


def by_col(move):
    def target(c):
        x, y, core = move(c // 8, (c // 2) % 4, c % 2)
        return x * 8 + (y % 4) * 2 + core

    return [(c, target(c)) for c in range(16)]


def z_pairs(second):
    pairs = []
    for r in range(16):
        for c in range(16):
            z = r % 8
            up = (z + c + second) % 2 == 0
            other = (r // 8) * 8 + (z + (1 if up else -1)) % 8
            pairs.append((r * 16 + c, other * 16 + c))
    return pairs


X_FAR = by_row(lambda x, z: (1 - x) * 8 + z)
OTHER_CORE = by_col(lambda x, y, k: (x, y, 1 - k))
Z_FIRST, Z_SECOND = z_pairs(0), z_pairs(1)
SAME_CORE = [[c for c in range(16) if c % 2 == k] for k in range(2)]


class Lane:
    def __init__(self):
        self.sent = []

    def after(self, value):
        if len(self.sent) >= IN_FLIGHT:
            value, _ = lax.optimization_barrier((value, self.sent[-IN_FLIGHT]))
        return value

    def send(self, value, axis, pairs):
        out = lax.ppermute(self.after(value), axis, pairs)
        self.sent.append(out)
        return out


class Ring:
    def __init__(self, lane, block):
        self.lane, self.got = lane, [block[None]]

    def step(self):
        at = len(self.got)
        payload = jnp.concatenate(self.got, 0) if at == 2 else self.got[-1]
        pairs = Z_FIRST if at % 2 else Z_SECOND
        self.got.append(self.lane.send(payload, ("row", "col"), pairs))


class Place:
    def __init__(self):
        row, col = lax.axis_index("row"), lax.axis_index("col")
        self.x, self.z, self.core = row // 8, row % 8, col % 2
        self.sign = 1 - 2 * ((self.z + col) % 2)

    def rows(self, x_major):
        order = [(f, d) for f in (0, 1) for d in ARRIVAL]
        if not x_major:
            order = [(f, d) for d in ARRIVAL for f in (0, 1)]
        return [((self.x + f) % 2) * 8 + (self.z + self.sign * d + 8) % 8 for f, d in order]


def input_grad_parts(pieces, weight, place, spans):
    n, width, depth = len(pieces), weight.shape[1], weight.shape[0]
    steps = width // INPUT_TILE
    tokens = sum(p.shape[0] for p in pieces)
    where = [(r % 2, r // 2) for r in place.rows(True)]
    keep = jnp.stack([jnp.where(core == place.core, 1, 0) for core, _ in where])
    slot = jnp.stack([at for _, at in where])

    def kernel(keep_ref, slot_ref, *refs):
        piece_refs, weight_ref, mine_ref, other_ref, total = refs[:n], refs[n], refs[n + 1], refs[n + 2], refs[n + 3]
        step = pl.program_id(0)
        block = jnp.concatenate([ref[...] for ref in piece_refs], 0)
        product = dot(block, weight_ref[...], ((1,), (1,)))

        @pl.when(step == 0)
        def _():
            total[...] = product

        @pl.when(step > 0)
        def _():
            total[...] += product

        @pl.when(step == steps - 1)
        def _():
            at = 0
            for index, (first, last) in enumerate(spans):
                found = slice(at, at + last - first)
                at += last - first
                for ref, wanted in ((mine_ref, 1), (other_ref, 0)):

                    @pl.when(keep_ref[index % 16] == wanted)
                    def _():
                        ref[slot_ref[index % 16], first:last] = total[found]

    rows = tokens // 16
    half = jax.ShapeDtypeStruct((8, rows, depth), F32)
    whole = pl.BlockSpec((8, rows, depth), lambda k, *_: (0, 0, 0))
    return pl.pallas_call(
        kernel,
        out_shape=(half, half),
        grid_spec=pltpu.PrefetchScalarGridSpec(
            num_scalar_prefetch=2,
            grid=(steps,),
            in_specs=[pl.BlockSpec((p.shape[0], INPUT_TILE), lambda k, *_: (0, k)) for p in pieces]
            + [pl.BlockSpec((depth, INPUT_TILE), lambda k, *_: (0, k))],
            out_specs=(whole, whole),
            scratch_shapes=[pltpu.VMEM((tokens, depth), F32)],
        ),
        compiler_params=pltpu.CompilerParams(vmem_limit_bytes=VMEM_LIMIT),
        cost_estimate=pl.CostEstimate(flops=2 * tokens * width * depth, bytes_accessed=16 << 20, transcendentals=0),
    )(keep, slot, *pieces, weight)


def weight_grad(features, slots, pieces, rows):
    width, depth = pieces[0].shape[1], features.shape[2]
    tokens = sum(p.shape[0] for p in pieces)

    def kernel(slot_ref, features_ref, *refs):
        piece_refs, out_ref, sorted_ref = refs[:-2], refs[-2], refs[-1]

        @pl.when(pl.program_id(0) == 0)
        def _():
            at = 0
            for index, (first, last) in enumerate(rows):
                found = features_ref[slot_ref[index]]
                sorted_ref[at : at + last - first] = found[first:last]
                at += last - first

        block = jnp.concatenate([ref[...] for ref in piece_refs], 0)
        out_ref[...] = dot(sorted_ref[...], block, ((0,), (0,))).astype(BF16)

    return pl.pallas_call(
        kernel,
        out_shape=jax.ShapeDtypeStruct((depth, width), BF16),
        grid_spec=pltpu.PrefetchScalarGridSpec(
            num_scalar_prefetch=1,
            grid=(width // WEIGHT_TILE,),
            in_specs=[pl.BlockSpec(features.shape, lambda k, *_: (0, 0, 0))]
            + [pl.BlockSpec((p.shape[0], WEIGHT_TILE), lambda k, *_: (0, k)) for p in pieces],
            out_specs=pl.BlockSpec((depth, WEIGHT_TILE), lambda k, *_: (0, k)),
            scratch_shapes=[pltpu.VMEM((tokens, depth), BF16)],
        ),
        compiler_params=pltpu.CompilerParams(vmem_limit_bytes=VMEM_LIMIT),
        cost_estimate=pl.CostEstimate(flops=2 * depth * tokens * width, bytes_accessed=16 << 20, transcendentals=0),
    )(slots, features, *pieces)


def dot(a, b, dims):
    return lax.dot_general(a, b, (dims, ((), ())), preferred_element_type=F32)


def flat(pieces):
    return [pltpu.with_memory_space_constraint(piece.reshape(-1, piece.shape[-1]), pltpu.HBM) for piece in pieces]


def tie(value, *others):
    return lax.optimization_barrier((value, *others))[0]


def body(inputs, grad_out, weight):
    all_inputs = lax.all_gather(inputs, "col", axis=0, tiled=False)
    place, lane = Place(), Lane()
    cut = lambda k: grad_out[GROUPS[k][0] : GROUPS[k][1]]
    rings, rest = {"b": Ring(lane, cut("late")), "a": Ring(lane, cut("first"))}, []
    for op in ORDER:
        if op == "A":
            rings["f"] = Ring(lane, lane.send(cut("first"), "row", X_FAR))
        elif op == "B":
            rest.append(lane.send(rings["b"].got[len(rest)], "row", X_FAR))
        else:
            rings[op].step()
    pieces = rings["b"].got + rest + rings["a"].got + rings["f"].got
    all_inputs, *pieces = lax.optimization_barrier((all_inputs, *pieces))
    blocks = flat(pieces)
    spans = [GROUPS[k] for k in GROUPS for _ in range(16)]
    mine, other = input_grad_parts(blocks, weight, place, spans)
    mine = mine + lax.ppermute(other, "col", OTHER_CORE)
    total = lax.all_to_all(mine, "col", 0, 0, axis_index_groups=SAME_CORE)
    slots = jnp.stack(2 * place.rows(True))
    out = weight_grad(tie(all_inputs, mine), slots, blocks, spans)
    return out, jnp.sum(total, 0).astype(BF16)


def solution(mesh):
    in_specs = (P("col", "row"), P("row", "col"), P("row", "col"))
    out_specs = (P("row", "col"), P("col", "row"))
    return jax.shard_map(body, mesh=mesh, in_specs=in_specs, out_specs=out_specs, check_vma=False)
```

```python
import jax
import jax.numpy as jnp
from jax import lax
from jax.experimental import pallas as pl
from jax.experimental.pallas import tpu as pltpu
from jax.sharding import PartitionSpec as P

BF16, F32 = jnp.bfloat16, jnp.float32
ARRIVAL = (0, 1, -1, -2, 2, 3, -3, -4)
GROUPS = {"late": (0, 48), "first": (48, 96)}
ORDER = "AbBabBfabBfabBfafB"
IN_FLIGHT = 4
INPUT_TILE, WEIGHT_TILE, VMEM_LIMIT = 768, 512, 40 << 20


def by_row(move):
    return [(r, move(r // 8, r % 8)) for r in range(16)]


def by_col(move):
    def target(c):
        x, y, core = move(c // 8, (c // 2) % 4, c % 2)
        return x * 8 + (y % 4) * 2 + core

    return [(c, target(c)) for c in range(16)]


def z_pairs(second):
    pairs = []
    for r in range(16):
        for c in range(16):
            z = r % 8
            up = (z + c + second) % 2 == 0
            other = (r // 8) * 8 + (z + (1 if up else -1)) % 8
            pairs.append((r * 16 + c, other * 16 + c))
    return pairs


X_FAR = by_row(lambda x, z: (1 - x) * 8 + z)
OTHER_CORE = by_col(lambda x, y, k: (x, y, 1 - k))
Z_FIRST, Z_SECOND = z_pairs(0), z_pairs(1)
SAME_CORE = [[c for c in range(16) if c % 2 == k] for k in range(2)]


class Lane:
    def __init__(self):
        self.sent = []

    def after(self, value):
        if len(self.sent) >= IN_FLIGHT:
            value, _ = lax.optimization_barrier((value, self.sent[-IN_FLIGHT]))
        return value

    def send(self, value, axis, pairs):
        out = lax.ppermute(self.after(value), axis, pairs)
        self.sent.append(out)
        return out


class Ring:
    def __init__(self, lane, block):
        self.lane, self.got = lane, [block[None]]

    def step(self):
        at = len(self.got)
        payload = jnp.concatenate(self.got, 0) if at == 2 else self.got[-1]
        pairs = Z_FIRST if at % 2 else Z_SECOND
        self.got.append(self.lane.send(payload, ("row", "col"), pairs))


class Place:
    def __init__(self):
        row, col = lax.axis_index("row"), lax.axis_index("col")
        self.x, self.z, self.core = row // 8, row % 8, col % 2
        self.sign = 1 - 2 * ((self.z + col) % 2)

    def rows(self, x_major):
        order = [(f, d) for f in (0, 1) for d in ARRIVAL]
        if not x_major:
            order = [(f, d) for d in ARRIVAL for f in (0, 1)]
        return [((self.x + f) % 2) * 8 + (self.z + self.sign * d + 8) % 8 for f, d in order]


def input_grad_parts(pieces, weight, place, spans):
    n, width, depth = len(pieces), weight.shape[1], weight.shape[0]
    steps = width // INPUT_TILE
    tokens = sum(p.shape[0] for p in pieces)
    where = [(r % 2, r // 2) for r in place.rows(True)]
    keep = jnp.stack([jnp.where(core == place.core, 1, 0) for core, _ in where])
    slot = jnp.stack([at for _, at in where])

    def kernel(keep_ref, slot_ref, *refs):
        piece_refs, weight_ref, mine_ref, other_ref, total = refs[:n], refs[n], refs[n + 1], refs[n + 2], refs[n + 3]
        step = pl.program_id(0)
        block = jnp.concatenate([ref[...] for ref in piece_refs], 0)
        product = dot(block, weight_ref[...], ((1,), (1,)))

        @pl.when(step == 0)
        def _():
            total[...] = product

        @pl.when(step > 0)
        def _():
            total[...] += product

        @pl.when(step == steps - 1)
        def _():
            at = 0
            for index, (first, last) in enumerate(spans):
                found = slice(at, at + last - first)
                at += last - first
                for ref, wanted in ((mine_ref, 1), (other_ref, 0)):

                    @pl.when(keep_ref[index % 16] == wanted)
                    def _():
                        ref[slot_ref[index % 16], first:last] = total[found]

    rows = tokens // 16
    half = jax.ShapeDtypeStruct((8, rows, depth), F32)
    whole = pl.BlockSpec((8, rows, depth), lambda k, *_: (0, 0, 0))
    return pl.pallas_call(
        kernel,
        out_shape=(half, half),
        grid_spec=pltpu.PrefetchScalarGridSpec(
            num_scalar_prefetch=2,
            grid=(steps,),
            in_specs=[pl.BlockSpec((p.shape[0], INPUT_TILE), lambda k, *_: (0, k)) for p in pieces]
            + [pl.BlockSpec((depth, INPUT_TILE), lambda k, *_: (0, k))],
            out_specs=(whole, whole),
            scratch_shapes=[pltpu.VMEM((tokens, depth), F32)],
        ),
        compiler_params=pltpu.CompilerParams(vmem_limit_bytes=VMEM_LIMIT),
        cost_estimate=pl.CostEstimate(flops=2 * tokens * width * depth, bytes_accessed=16 << 20, transcendentals=0),
    )(keep, slot, *pieces, pltpu.with_memory_space_constraint(weight, pltpu.HBM))


def weight_grad(features, slots, pieces, rows):
    width, depth = pieces[0].shape[1], features.shape[2]
    tokens = sum(p.shape[0] for p in pieces)

    def kernel(slot_ref, features_ref, *refs):
        piece_refs, out_ref, sorted_ref = refs[:-2], refs[-2], refs[-1]

        @pl.when(pl.program_id(0) == 0)
        def _():
            at = 0
            for index, (first, last) in enumerate(rows):
                found = features_ref[slot_ref[index]]
                sorted_ref[at : at + last - first] = found[first:last]
                at += last - first

        block = jnp.concatenate([ref[...] for ref in piece_refs], 0)
        out_ref[...] = dot(sorted_ref[...], block, ((0,), (0,))).astype(BF16)

    return pl.pallas_call(
        kernel,
        out_shape=jax.ShapeDtypeStruct((depth, width), BF16),
        grid_spec=pltpu.PrefetchScalarGridSpec(
            num_scalar_prefetch=1,
            grid=(width // WEIGHT_TILE,),
            in_specs=[pl.BlockSpec(features.shape, lambda k, *_: (0, 0, 0))]
            + [pl.BlockSpec((p.shape[0], WEIGHT_TILE), lambda k, *_: (0, k)) for p in pieces],
            out_specs=pl.BlockSpec((depth, WEIGHT_TILE), lambda k, *_: (0, k)),
            scratch_shapes=[pltpu.VMEM((tokens, depth), BF16)],
        ),
        compiler_params=pltpu.CompilerParams(vmem_limit_bytes=VMEM_LIMIT),
        cost_estimate=pl.CostEstimate(flops=2 * depth * tokens * width, bytes_accessed=16 << 20, transcendentals=0),
    )(slots, features, *pieces)


def dot(a, b, dims):
    return lax.dot_general(a, b, (dims, ((), ())), preferred_element_type=F32)


def flat(pieces):
    return [pltpu.with_memory_space_constraint(piece.reshape(-1, piece.shape[-1]), pltpu.HBM) for piece in pieces]


def tie(value, *others):
    return lax.optimization_barrier((value, *others))[0]


def body(inputs, grad_out, weight):
    all_inputs = lax.all_gather(inputs, "col", axis=0, tiled=False)
    place, lane = Place(), Lane()
    cut = lambda k: grad_out[GROUPS[k][0] : GROUPS[k][1]]
    rings, rest = {"b": Ring(lane, cut("late")), "a": Ring(lane, cut("first"))}, []
    for op in ORDER:
        if op == "A":
            rings["f"] = Ring(lane, lane.send(cut("first"), "row", X_FAR))
        elif op == "B":
            rest.append(lane.send(rings["b"].got[len(rest)], "row", X_FAR))
        else:
            rings[op].step()
    pieces = rings["b"].got + rest + rings["a"].got + rings["f"].got
    pieces = lax.optimization_barrier(pieces)
    blocks = flat(pieces)
    spans = [GROUPS[k] for k in GROUPS for _ in range(16)]
    mine, other = input_grad_parts(blocks, weight, place, spans)
    mine = mine + lax.ppermute(other, "col", OTHER_CORE)
    total = lax.all_to_all(mine, "col", 0, 0, axis_index_groups=SAME_CORE)
    slots = jnp.stack(2 * place.rows(True))
    out = weight_grad(tie(all_inputs, mine), slots, blocks, spans)
    return out, jnp.sum(total, 0).astype(BF16)


def solution(mesh):
    in_specs = (P("col", "row"), P("row", "col"), P("row", "col"))
    out_specs = (P("row", "col"), P("col", "row"))
    return jax.shard_map(body, mesh=mesh, in_specs=in_specs, out_specs=out_specs, check_vma=False)
```
